256 devices in a mesh: replica: 16 (over y_hi, z), tensor: 16 (over x, y_lo, core).
Axes of the slice: x: 4, y: 4 (y_hi: 2, y_lo: 2; y = y_hi * 2 + y_lo), z: 8, core: 2. Of those that a mesh axis runs over, the one named last changes fastest.
Arguments:
- tokens_in: bfloat16 [8192, 2048], P(('replica', 'tensor')), may hold values from -6 to 6
- cotangent: bfloat16 [8192, 2048], P(('replica', 'tensor')), may hold values from -6 to 6
- gate_weight: bfloat16 [32768, 7168], P('replica', 'tensor'), may hold values from -6 to 6
- up_weight: bfloat16 [32768, 7168], P('replica', 'tensor'), may hold values from -6 to 6
- down_weight: bfloat16 [114688, 2048], P(('replica', 'tensor')), may hold values from -6 to 6
- step_index: int32 [1], replicated, may hold values from 0 to 63
Outputs:
- mixed_gate: bfloat16 [32768, 7168], P('replica', 'tensor')
- mixed_up: bfloat16 [32768, 7168], P('replica', 'tensor')
- mixed_down: bfloat16 [114688, 2048], P(('replica', 'tensor'))
- layer_out: bfloat16 [8192, 2048], P(('replica', 'tensor'))
- d_tokens: bfloat16 [8192, 2048], P(('replica', 'tensor'))
The draws below stay inside these ranges and needn't reach their ends.
All inputs are finite; a program needn't handle non-finite values.
Results may differ from the reference program's by a relative error of at most 0.0065.
Values may be sent and summed in bfloat16 or wider, within the bound.
A program may use at most 128 MiB of HBM per device.

```python
import jax
import jax.numpy as jnp
from jax import lax

D = 2048
FF = 7168
TOK = 512
HOPS = 4
ROWS = 8192
DROWS = 32768
FROWS = 114688
N_REPLICA = 16


def levels(key, extent, split, smallest, largest):
    def one(dim, blocks):
        heights = jax.random.uniform(jax.random.fold_in(jax.random.fold_in(key, 6), dim), (blocks,), jnp.float32, smallest / len(split), largest / len(split))
        return jnp.repeat(jnp.exp(heights), extent[dim] // blocks).reshape((-1,) + (1,) * (len(extent) - dim - 1))

    gain = one(*split[0])
    for cut in split[1:]:
        gain = gain * one(*cut)
    return gain


def centred(rng, dims, scale, bound, shards=(), kind=jnp.bfloat16):
    values = scale * jax.random.normal(rng, dims, jnp.float32)
    if shards:
        values = values * levels(rng, dims, shards, -0.22, 0.18)
    return jnp.clip(values, -bound, bound).astype(kind)


def setup_inputs(seed: int = 0) -> dict:
    key_of = jax.random.split(jax.random.key(seed), 7)
    return {
        "tokens_in": centred(key_of[0], (ROWS, D), 1.0, 6.0, ((0, 256),)),
        "cotangent": centred(key_of[1], (ROWS, D), 1.0, 6.0, ((0, 256),)),
        "gate_weight": centred(key_of[2], (DROWS, FF), 1.0, 6.0, ((0, 16), (1, 16))),
        "up_weight": centred(key_of[3], (DROWS, FF), 1.0, 6.0, ((0, 16), (1, 16))),
        "down_weight": centred(key_of[4], (FROWS, D), 1.0, 6.0, ((0, 256),)),
        "step_index": jax.random.randint(key_of[5], (1,), 0, 64).astype(jnp.int32),
    }


epsilon = 1e-05
learning_rate = 2.0

def replica_step(pack):
    tokens_in, cotangent, gate_weight, up_weight, down_weight = pack
    scale_model = D ** (-0.5)
    scale_hidden = FF ** (-0.5)
    tokens_f32 = tokens_in.astype(jnp.float32)
    inverse_rms = lax.rsqrt(lax.optimization_barrier(jnp.mean(tokens_f32 * tokens_f32, axis=-1, keepdims=True)) + epsilon)
    normal_f = tokens_f32 * inverse_rms
    normed = normal_f.astype(jnp.bfloat16)
    gate_pre = jnp.dot(normed, gate_weight, preferred_element_type=jnp.float32) * scale_model
    up_pre = jnp.dot(normed, up_weight, preferred_element_type=jnp.float32) * scale_model
    gate_sigmoid = jax.nn.sigmoid(gate_pre)
    hidden = (gate_pre * gate_sigmoid * up_pre).astype(jnp.bfloat16)
    layer_out = (jnp.dot(hidden, down_weight, preferred_element_type=jnp.float32) * scale_hidden).astype(jnp.bfloat16)
    d_hidden = jnp.dot(cotangent, down_weight.T, preferred_element_type=jnp.float32) * scale_hidden
    d_gate = (d_hidden * up_pre * gate_sigmoid * (1.0 + gate_pre * (1.0 - gate_sigmoid))).astype(jnp.bfloat16)
    d_up = (d_hidden * gate_pre * gate_sigmoid).astype(jnp.bfloat16)
    grad_down = jnp.dot(hidden.T, cotangent, preferred_element_type=jnp.float32) * scale_hidden
    grad_gate = jnp.dot(normed.T, d_gate, preferred_element_type=jnp.float32) * scale_model
    grad_up = jnp.dot(normed.T, d_up, preferred_element_type=jnp.float32) * scale_model
    new_gate = (gate_weight.astype(jnp.float32) - learning_rate * grad_gate).astype(jnp.bfloat16)
    new_up = (up_weight.astype(jnp.float32) - learning_rate * grad_up).astype(jnp.bfloat16)
    new_down = (down_weight.astype(jnp.float32) - learning_rate * grad_down).astype(jnp.bfloat16)
    d_normed = (jnp.dot(d_gate, gate_weight.T, preferred_element_type=jnp.float32) + jnp.dot(d_up, up_weight.T, preferred_element_type=jnp.float32)) * scale_model
    inner = lax.optimization_barrier(jnp.mean(d_normed * normal_f, axis=-1, keepdims=True))
    d_tokens = (inverse_rms * (d_normed - normal_f * inner)).astype(jnp.bfloat16)
    return (new_gate, new_up, new_down, layer_out, d_tokens)

def reference(tokens_in, cotangent, gate_weight, up_weight, down_weight, step_index):
    stacked = (tokens_in.reshape(N_REPLICA, TOK, D), cotangent.reshape(N_REPLICA, TOK, D), gate_weight.reshape(N_REPLICA, D, FF), up_weight.reshape(N_REPLICA, D, FF), down_weight.reshape(N_REPLICA, FF, D))
    new_gate, new_up, new_down, layer_out, d_tokens = lax.map(replica_step, stacked)
    bit_now = (step_index[0] % HOPS).astype(jnp.int32)
    partner = jnp.bitwise_xor(jnp.arange(N_REPLICA, dtype=jnp.int32), jnp.left_shift(jnp.int32(1), bit_now)).astype(jnp.int32)

    def mixing(updated):
        other = jnp.take(updated, partner, axis=0)
        return (0.5 * (updated.astype(jnp.float32) + other.astype(jnp.float32))).astype(jnp.bfloat16)
    mixed_gate = mixing(new_gate).reshape(N_REPLICA * D, FF)
    mixed_up = mixing(new_up).reshape(N_REPLICA * D, FF)
    mixed_down = mixing(new_down).reshape(N_REPLICA * FF, D)
    return (mixed_gate, mixed_up, mixed_down, layer_out.reshape(N_REPLICA * TOK, D), d_tokens.reshape(N_REPLICA * TOK, D))
```

```python
import functools

import jax
import jax.numpy as jnp
from jax import lax
from jax.experimental import pallas as pl
from jax.experimental.pallas import tpu as pltpu
from jax.sharding import PartitionSpec as P

D = 2048
FF = 7168
EPSILON = 1e-05
RATE = 2.0
MODEL = D ** (-0.5)
HIDDEN = FF ** (-0.5)

TOK = 512
OWN = 32
PAIR = 64
ROWS = 448
STEP = 64
BLOCKS = ROWS // STEP
COLS = 256

MESH = pl.DeviceIdType.MESH
ANY = pl.BlockSpec(memory_space=pl.ANY)

RAW = (192, 128, 128, 192)


def dot(a, b, dims):
    return lax.dot_general(a, b, (dims, ((), ())), preferred_element_type=jnp.float32)


LAST = ((1,), (1,))
PLAIN = ((1,), (0,))
FIRST = ((0,), (0,))


def kernel(
    k, raw,
    tok, cot, gate, up, down,
    newo, newp, lo, dt,
    tok_v, norm_v, gath, wv, newv, praw, pnew,
    act_a, act_b, hid, d_gu, part, got, ysend, yrecv, lo_v, dt_v,
    load_sem, store_sem,
    gy_s, gy_r, gx_s, gx_r, gc_s, gc_r,
    r_s, r_r, ry_s, ry_r,
    zt_s, zt_r, zraw_s, zraw_r, znew_s, znew_r,
):
    rep, ten = lax.axis_index("replica"), lax.axis_index("tensor")
    core, y, x = lax.rem(ten, 2), lax.rem(ten // 2, 2), ten // 4
    bit = lax.rem(rep // (1 << k), 2)
    partner = (rep + (1 << k) - (2 << k) * bit, ten)
    across = (rep, ten + 2 - 4 * y)
    sibling = (rep, ten + 1 - 2 * core)

    def along_x(j):
        return (rep, lax.rem(x + j, 4) * 4 + y * 2 + core)

    def plane(j):
        q = lax.rem(core * 4 + x + j, 8)
        return (rep, lax.rem(q, 4) * 4 + y * 2 + q // 4)

    def pair_rows(c, xx):
        return pl.ds(pl.multiple_of((c * 4 + xx) * PAIR, PAIR), PAIR)

    own_rows = pl.ds(pl.multiple_of((core * 4 + x) * PAIR + y * OWN, OWN), OWN)

    def remote(src, dst, send, recv, device):
        return pltpu.make_async_remote_copy(
            src_ref=src, dst_ref=dst, send_sem=send, recv_sem=recv, device_id=device, device_id_type=MESH
        )

    load_tok = pltpu.make_async_copy(tok, tok_v, load_sem.at[0])
    load_cot = pltpu.make_async_copy(cot, gath.at[1, own_rows], load_sem.at[1])
    load_w = [
        pltpu.make_async_copy(ref, wv.at[i], load_sem.at[2 + i]) for i, ref in enumerate((gate, up, down))
    ]
    load_tok.start()
    load_cot.start()
    for c in load_w:
        c.start()

    barrier = pltpu.get_barrier_semaphore()
    for device in [partner, across] + [plane(j) for j in range(1, 8)]:
        pl.semaphore_signal(barrier, inc=1, device_id=device, device_id_type=MESH)

    load_tok.wait()
    value = tok_v[...].astype(jnp.float32)
    inverse = lax.rsqrt(jnp.mean(value * value, axis=-1, keepdims=True) + EPSILON)
    norm_v[...] = value * inverse
    gath[0, own_rows, :] = norm_v[...].astype(jnp.bfloat16)
    load_cot.wait()

    pl.semaphore_wait(barrier, 9)

    def y_copy(a):
        return remote(gath.at[a, own_rows], gath.at[a, own_rows], gy_s.at[a], gy_r.at[a], across)

    def x_copy(a, j):
        rows = pair_rows(core, x)
        return remote(gath.at[a, rows], gath.at[a, rows], gx_s.at[a, j], gx_r.at[a, j], along_x(j))

    def c_copy(a, j):
        rows = pair_rows(core, lax.rem(x + 4 - j, 4))
        return remote(gath.at[a, rows], gath.at[a, rows], gc_s.at[a, j], gc_r.at[a, j], sibling)

    def spread(a):
        y_copy(a).wait_recv()
        for j in (1, 3, 2):
            x_copy(a, j).start()
        c_copy(a, 0).start()

    def pass_on(a):
        for j in (1, 3, 2):
            x_copy(a, j).wait_recv()
            c_copy(a, j).start()

    def gathered(a):
        for j in range(4):
            c_copy(a, j).wait_recv()

    y_copy(0).start()
    y_copy(1).start()

    def z_tok(a):
        return remote(gath.at[a, own_rows], gath.at[a + 2, own_rows], zt_s.at[a], zt_r.at[a], partner)

    def z_raw(i):
        ref = (gate, up, down)[i]
        return remote(ref.at[pl.ds(0, raw)], praw.at[i], zraw_s.at[i], zraw_r.at[i], partner)

    def block(b):
        return pl.ds(pl.multiple_of(b * STEP, STEP), STEP)

    def z_new(b):
        return remote(newv.at[:, block(b)], newp.at[:, block(b)], znew_s.at[b], znew_r.at[b], partner)

    def store_own(b):
        return pltpu.make_async_copy(newv.at[:, block(b)], newo.at[:, block(b)], store_sem.at[b])

    def store_partner(b):
        return pltpu.make_async_copy(pnew.at[:, block(b)], newp.at[:, block(b)], store_sem.at[BLOCKS + b])

    z_tok(0).start()
    z_tok(1).start()
    for i in range(3):
        z_raw(i).start()

    spread(0)
    spread(1)
    pass_on(0)
    gathered(0)
    for c in load_w:
        c.wait()

    def forward(w, base, b):
        rows = block(b)
        gate_pre = dot(w[0, rows, :], gath[base], LAST) * MODEL
        up_pre = dot(w[1, rows, :], gath[base], LAST) * MODEL
        s = jax.nn.sigmoid(gate_pre)
        silu = gate_pre * s
        hid[rows, :] = (silu * up_pre).astype(jnp.bfloat16)
        act_a[rows, :] = up_pre * s * (1.0 + gate_pre * (1.0 - s))
        act_b[rows, :] = silu

    def backward(w, new, base, b):
        rows = block(b)
        d_hidden = dot(w[2, rows, :], gath[base + 1], LAST) * HIDDEN
        d_gu[0, rows, :] = (d_hidden * act_a[rows, :]).astype(jnp.bfloat16)
        d_gu[1, rows, :] = (d_hidden * act_b[rows, :]).astype(jnp.bfloat16)
        for i, (left, right, scale) in enumerate(
            ((d_gu.at[0], base, MODEL), (d_gu.at[1], base, MODEL), (hid, base + 1, HIDDEN))
        ):
            grad = dot(left[rows, :], gath[right], PLAIN) * scale
            new[i, rows, :] = (w[i, rows, :].astype(jnp.float32) - RATE * grad).astype(jnp.bfloat16)

    def loop(low, high, step):
        if high > low:
            lax.fori_loop(low, high, lambda b, _: (step(b), 0)[1], 0)

    loop(0, BLOCKS, lambda b: forward(wv, 0, b))
    pass_on(1)

    def r_copy(n, j):
        q = lax.rem(core * 4 + x + j, 8)
        rows = pl.ds(pl.multiple_of(q * PAIR, PAIR), PAIR)
        return remote(part.at[n, rows], got.at[n, j], r_s.at[n, j], r_r.at[n, j], plane(j))

    def layer(n):
        cols = pl.ds(pl.multiple_of(n * COLS, COLS), COLS)
        part[0, :, cols] = dot(hid[...], wv[2, :, cols], FIRST).astype(jnp.bfloat16)

    loop(0, D // COLS, layer)
    for j in range(1, 8):
        r_copy(0, j).start()

    gathered(1)
    for a in (0, 1):
        z_tok(a).wait_recv()
        y_copy(a + 2).start()

    first = raw // STEP

    def update_and_send(b):
        backward(wv, newv, 0, b)
        z_new(b).start()
        store_own(b).start()

    def update(b):
        backward(wv, newv, 0, b)
        store_own(b).start()

    loop(first, BLOCKS, update_and_send)
    spread(2)
    spread(3)
    loop(0, first, update)

    def back_to_input(n):
        cols = pl.ds(pl.multiple_of(n * COLS, COLS), COLS)
        total = dot(d_gu[0], wv[0, :, cols], FIRST) + dot(d_gu[1], wv[1, :, cols], FIRST)
        part[1, :, cols] = total.astype(jnp.bfloat16)

    loop(0, D // COLS, back_to_input)
    for j in range(1, 8):
        r_copy(1, j).start()
    pass_on(2)
    pass_on(3)

    mine = pl.ds(pl.multiple_of(y * OWN, OWN), OWN)
    other = pl.ds(pl.multiple_of(OWN - y * OWN, OWN), OWN)

    def ry_copy(n):
        return remote(ysend.at[n], yrecv.at[n], ry_s.at[n], ry_r.at[n], across)

    def plane_sum(n, half):
        start = pl.multiple_of((core * 4 + x) * PAIR + half * OWN, OWN)
        total = part[n, pl.ds(start, OWN), :].astype(jnp.float32)
        rows = mine if half is y else other
        for j in range(1, 8):
            total = total + got[n, j, rows, :].astype(jnp.float32)
        return total

    for n in (0, 1):
        for j in range(1, 8):
            r_copy(n, j).wait_recv()
        ysend[n] = plane_sum(n, 1 - y).astype(jnp.bfloat16)
        ry_copy(n).start()

    for a in (2, 3):
        gathered(a)
    for i in range(3):
        z_raw(i).wait_recv()

    def redo(b):
        forward(praw, 2, b)
        backward(praw, pnew, 2, b)
        store_partner(b).start()

    loop(0, first, redo)

    ry_copy(0).wait_recv()
    lo_v[...] = ((plane_sum(0, y) + yrecv[0].astype(jnp.float32)) * HIDDEN).astype(jnp.bfloat16)
    store_lo = pltpu.make_async_copy(lo_v, lo, load_sem.at[0])
    store_lo.start()
    ry_copy(1).wait_recv()
    d_normed = (plane_sum(1, y) + yrecv[1].astype(jnp.float32)) * MODEL
    inner = jnp.mean(d_normed * norm_v[...], axis=-1, keepdims=True)
    value = tok_v[...].astype(jnp.float32)
    inverse = lax.rsqrt(jnp.mean(value * value, axis=-1, keepdims=True) + EPSILON)
    dt_v[...] = (inverse * (d_normed - norm_v[...] * inner)).astype(jnp.bfloat16)
    store_dt = pltpu.make_async_copy(dt_v, dt, load_sem.at[1])
    store_dt.start()

    store_lo.wait()
    store_dt.wait()
    loop(0, BLOCKS, lambda b: store_own(b).wait())
    loop(0, first, lambda b: store_partner(b).wait())
    for a in range(4):
        y_copy(a).wait_send()
        for j in range(1, 4):
            x_copy(a, j).wait_send()
        for j in range(4):
            c_copy(a, j).wait_send()
    for n in (0, 1):
        for j in range(1, 8):
            r_copy(n, j).wait_send()
        ry_copy(n).wait_send()
        z_tok(n).wait_send()
    for i in range(3):
        z_raw(i).wait_send()
    loop(first, BLOCKS, lambda b: z_new(b).wait())


def exchange(k, tok, cot, gate, up, down):
    raw = RAW[k]
    bf, f32 = jnp.bfloat16, jnp.float32
    dma = pltpu.SemaphoreType.DMA
    stacked = jax.ShapeDtypeStruct((3, ROWS, D), bf)
    small = jax.ShapeDtypeStruct((OWN, D), bf)
    return pl.pallas_call(
        functools.partial(kernel, k, raw),
        out_shape=(stacked, stacked, small, small),
        in_specs=[ANY] * 5,
        out_specs=(ANY,) * 4,
        scratch_shapes=[
            pltpu.VMEM((OWN, D), bf),
            pltpu.VMEM((OWN, D), f32),
            pltpu.VMEM((4, TOK, D), bf),
            pltpu.VMEM((3, ROWS, D), bf),
            pltpu.VMEM((3, ROWS, D), bf),
            pltpu.VMEM((3, raw, D), bf),
            pltpu.VMEM((3, raw, D), bf),
            pltpu.VMEM((ROWS, TOK), f32),
            pltpu.VMEM((ROWS, TOK), f32),
            pltpu.VMEM((ROWS, TOK), bf),
            pltpu.VMEM((2, ROWS, TOK), bf),
            pltpu.VMEM((2, TOK, D), bf),
            pltpu.VMEM((2, 8, PAIR, D), bf),
            pltpu.VMEM((2, OWN, D), bf),
            pltpu.VMEM((2, OWN, D), bf),
            pltpu.VMEM((OWN, D), bf),
            pltpu.VMEM((OWN, D), bf),
            dma((5,)),
            dma((2 * BLOCKS,)),
            dma((4,)),
            dma((4,)),
            dma((4, 4)),
            dma((4, 4)),
            dma((4, 4)),
            dma((4, 4)),
            dma((2, 8)),
            dma((2, 8)),
            dma((2,)),
            dma((2,)),
            dma((2,)),
            dma((2,)),
            dma((3,)),
            dma((3,)),
            dma((BLOCKS,)),
            dma((BLOCKS,)),
        ],
        compiler_params=pltpu.CompilerParams(
            collective_id=k, has_side_effects=True, vmem_limit_bytes=56 * 1024 * 1024
        ),
        name=f"exchange_{k}",
    )(tok, cot, gate, up, down)


def mix_kernel(own, theirs, lo, dt, gate, up, down, lo_out, dt_out):
    for i, out in enumerate((gate, up, down)):
        total = own[i].astype(jnp.float32) + theirs[i].astype(jnp.float32)
        out[...] = (0.5 * total).astype(jnp.bfloat16)
    lo_out[...] = lo[...]
    dt_out[...] = dt[...]


def mix(own, theirs, lo, dt):
    stacked = pl.BlockSpec((3, STEP, D), lambda i: (0, i, 0))
    one = pl.BlockSpec((STEP, D), lambda i: (i, 0))
    small = pl.BlockSpec((OWN, D), lambda i: (0, 0))
    weight = jax.ShapeDtypeStruct((ROWS, D), jnp.bfloat16)
    few = jax.ShapeDtypeStruct((OWN, D), jnp.bfloat16)
    return pl.pallas_call(
        mix_kernel,
        out_shape=(weight, weight, weight, few, few),
        grid=(BLOCKS,),
        in_specs=[stacked, stacked, small, small],
        out_specs=(one, one, one, small, small),
        compiler_params=pltpu.CompilerParams(vmem_limit_bytes=24 * 1024 * 1024),
        name="mix",
    )(own, theirs, lo, dt)


def body(tokens_in, cotangent, gate_weight, up_weight, down_weight, step_index):
    k = step_index[0] % 4
    branches = [functools.partial(exchange, n) for n in range(4)]
    own, theirs, lo, dt = lax.switch(k, branches, tokens_in, cotangent, gate_weight.T, up_weight.T, down_weight)
    gate, up, down, lo, dt = mix(own, theirs, lo, dt)
    return gate.T, up.T, down, lo, dt


def solution(mesh):
    rows = P(("replica", "tensor"), None)
    split = P("replica", "tensor")
    return jax.shard_map(
        body,
        mesh=mesh,
        in_specs=(rows, rows, split, split, rows, P()),
        out_specs=(split, split, rows, rows, rows),
        check_vma=False,
    )
```

```python
import functools

import jax
import jax.numpy as jnp
from jax import lax
from jax.experimental import pallas as pl
from jax.experimental.pallas import tpu as pltpu
from jax.sharding import PartitionSpec as P

D = 2048
FF = 7168
EPSILON = 1e-05
RATE = 2.0
MODEL = D ** (-0.5)
HIDDEN = FF ** (-0.5)

TOK = 512
OWN = 32
PAIR = 64
ROWS = 448
STEP = 64
BLOCKS = ROWS // STEP
HALF = STEP // 2
COLS = 256

MESH = pl.DeviceIdType.MESH
ANY = pl.BlockSpec(memory_space=pl.ANY)
HBM = pl.BlockSpec(memory_space=pltpu.HBM)
VMEM = pl.BlockSpec(memory_space=pltpu.VMEM)

RAW = (192, 128, 128, 256)
HELD = (0, 0, 0, 3)


def dot(a, b, dims):
    return lax.dot_general(a, b, (dims, ((), ())), preferred_element_type=jnp.float32)


LAST = ((1,), (1,))
PLAIN = ((1,), (0,))
FIRST = ((0,), (0,))


def kernel(
    k, raw,
    tok, cot, gate, up, down,
    mixed_gate, mixed_up, mixed_down, lo, dt,
    tok_v, norm_v, gath, wv, newv, praw, pnew,
    act_a, act_b, hid, d_gu, part, half, got, ysend, yrecv, lo_v, dt_v,
    load_sem, store_sem,
    gy_s, gy_r, gx_s, gx_r, gc_s, gc_r,
    rc_s, rc_r, rx_s, rx_r, ry_s, ry_r,
    zt_s, zt_r, zraw_s, zraw_r, znew_s, znew_r,
):
    rep, ten = lax.axis_index("replica"), lax.axis_index("tensor")
    core, y, x = lax.rem(ten, 2), lax.rem(ten // 2, 2), ten // 4
    bit = lax.rem(rep // (1 << k), 2)
    partner = (rep + (1 << k) - (2 << k) * bit, ten)
    across = (rep, ten + 2 - 4 * y)
    sibling = (rep, ten + 1 - 2 * core)
    mixed = (mixed_gate, mixed_up, mixed_down)

    def along_x(j):
        return (rep, lax.rem(x + j, 4) * 4 + y * 2 + core)

    def pair_rows(c, xx):
        return pl.ds(pl.multiple_of((c * 4 + xx) * PAIR, PAIR), PAIR)

    own_rows = pl.ds(pl.multiple_of((core * 4 + x) * PAIR + y * OWN, OWN), OWN)

    def remote(src, dst, send, recv, device):
        return pltpu.make_async_remote_copy(
            src_ref=src, dst_ref=dst, send_sem=send, recv_sem=recv, device_id=device, device_id_type=MESH
        )

    load_tok = pltpu.make_async_copy(tok, tok_v, load_sem.at[0])
    load_cot = pltpu.make_async_copy(cot, gath.at[1, own_rows], load_sem.at[1])
    load_w = [
        pltpu.make_async_copy(ref, wv.at[i], load_sem.at[2 + i]) for i, ref in enumerate((gate, up, down))
    ]
    barrier = pltpu.get_barrier_semaphore()
    friends = [partner, across, sibling] + [along_x(j) for j in (1, 2, 3)]
    for device in friends:
        pl.semaphore_signal(barrier, inc=1, device_id=device, device_id_type=MESH)
    load_tok.start()
    load_cot.start()
    for c in load_w:
        c.start()
    pl.semaphore_wait(barrier, len(friends))

    def z_raw(i, b):
        ref, rows = (gate, up, down)[i], pl.ds(b * STEP, STEP)
        return remote(ref.at[rows], praw.at[i, rows], zraw_s.at[i, b], zraw_r.at[i, b], partner)

    first = raw // STEP
    raws = [z_raw(i, b) for b in range(first) for i in range(3)]
    for c in raws[:3]:
        c.start()

    load_tok.wait()
    value = tok_v[...].astype(jnp.float32)
    inverse = lax.rsqrt(jnp.mean(value * value, axis=-1, keepdims=True) + EPSILON)
    norm_v[...] = value * inverse
    gath[0, own_rows, :] = norm_v[...].astype(jnp.bfloat16)
    load_cot.wait()

    def y_copy(a):
        return remote(gath.at[a, own_rows], gath.at[a, own_rows], gy_s.at[a], gy_r.at[a], across)

    def x_copy(a, j):
        rows = pair_rows(core, x)
        return remote(gath.at[a, rows], gath.at[a, rows], gx_s.at[a, j], gx_r.at[a, j], along_x(j))

    def c_copy(a, j):
        rows = pair_rows(core, lax.rem(x + 4 - j, 4))
        return remote(gath.at[a, rows], gath.at[a, rows], gc_s.at[a, j], gc_r.at[a, j], sibling)

    def spread(a):
        y_copy(a).wait_recv()
        for j in (1, 3, 2):
            x_copy(a, j).start()
        c_copy(a, 0).start()

    def pass_on(a):
        for j in (1, 3, 2):
            x_copy(a, j).wait_recv()
            c_copy(a, j).start()

    def gathered(a):
        for j in range(4):
            c_copy(a, j).wait_recv()

    y_copy(0).start()
    y_copy(1).start()

    def z_tok(a):
        return remote(gath.at[a, own_rows], gath.at[a + 2, own_rows], zt_s.at[a], zt_r.at[a], partner)

    def block(b):
        return pl.ds(pl.multiple_of(b * STEP, STEP), STEP)

    def piece(q, low=0):
        return pl.ds(pl.multiple_of(q * HALF - low, HALF), HALF)

    def z_new(q):
        return remote(newv.at[:, piece(q)], pnew.at[:, piece(q, raw)], znew_s.at[q], znew_r.at[q], partner)

    def store(i, ref, low, q):
        return pltpu.make_async_copy(ref.at[i, piece(q, low)], mixed[i].at[piece(q)], store_sem.at[i, q])

    z_tok(0).start()
    z_tok(1).start()
    for c in raws[3:]:
        c.start()
    spread(0)
    spread(1)
    pass_on(0)
    gathered(0)
    for c in load_w:
        c.wait()

    def forward(w, base, b):
        rows = block(b)
        gate_pre = dot(w[0, rows, :], gath[base], LAST) * MODEL
        up_pre = dot(w[1, rows, :], gath[base], LAST) * MODEL
        s = jax.nn.sigmoid(gate_pre)
        silu = gate_pre * s
        hid[rows, :] = (silu * up_pre).astype(jnp.bfloat16)
        act_a[rows, :] = up_pre * s * (1.0 + gate_pre * (1.0 - s))
        act_b[rows, :] = silu

    def backward(w, base, b, keep):
        rows = block(b)
        d_hidden = dot(w[2, rows, :], gath[base + 1], LAST) * HIDDEN
        d_gu[0, rows, :] = (d_hidden * act_a[rows, :]).astype(jnp.bfloat16)
        d_gu[1, rows, :] = (d_hidden * act_b[rows, :]).astype(jnp.bfloat16)
        for i, (left, right, scale) in enumerate(
            ((d_gu.at[0], base, MODEL), (d_gu.at[1], base, MODEL), (hid, base + 1, HIDDEN))
        ):
            grad = dot(left[rows, :], gath[right], PLAIN) * scale
            keep(i, rows, (w[i, rows, :].astype(jnp.float32) - RATE * grad).astype(jnp.bfloat16))

    def keep_own(i, rows, new):
        newv[i, rows, :] = new

    def mean(a, b):
        return (0.5 * (a.astype(jnp.float32) + b.astype(jnp.float32))).astype(jnp.bfloat16)

    def loop(low, high, step):
        if high > low:
            lax.fori_loop(low, high, lambda b, _: (step(b), 0)[1], 0)

    loop(0, BLOCKS, lambda b: forward(wv, 0, b))
    pass_on(1)

    def core_rows(c):
        return pl.ds(pl.multiple_of(c * (TOK // 2), TOK // 2), TOK // 2)

    def rc_copy(n):
        return remote(part.at[n, core_rows(1 - core)], half.at[n], rc_s.at[n], rc_r.at[n], sibling)

    def rx_copy(n, j):
        rows = pair_rows(core, lax.rem(x + j, 4))
        return remote(part.at[n, rows], got.at[n, j], rx_s.at[n, j], rx_r.at[n, j], along_x(j))

    def sum_cores(n):
        rc_copy(n).wait_recv()
        rows = core_rows(core)
        total = part[n, rows, :].astype(jnp.float32) + half[n].astype(jnp.float32)
        part[n, rows, :] = total.astype(jnp.bfloat16)
        for j in (2, 1, 3):
            rx_copy(n, j).start()

    def layer(n):
        cols = pl.ds(pl.multiple_of(n * COLS, COLS), COLS)
        part[0, :, cols] = dot(hid[...], wv[2, :, cols], FIRST).astype(jnp.bfloat16)

    loop(0, D // COLS, layer)
    rc_copy(0).start()

    gathered(1)

    def send(b):
        z_new(2 * b).start()
        z_new(2 * b + 1).start()

    def update_and_send(b):
        backward(wv, 0, b, keep_own)
        send(b)

    def partner_tokens():
        for a in (0, 1):
            z_tok(a).wait_recv()
            y_copy(a + 2).start()

    last = BLOCKS - HELD[k]
    if k == 3:
        partner_tokens()
    loop(first, last, update_and_send)
    loop(last, BLOCKS, lambda b: backward(wv, 0, b, keep_own))
    sum_cores(0)
    if k != 3:
        partner_tokens()
    loop(0, first, lambda b: backward(wv, 0, b, keep_own))

    def back_to_input(n):
        cols = pl.ds(pl.multiple_of(n * COLS, COLS), COLS)
        total = dot(d_gu[0], wv[0, :, cols], FIRST) + dot(d_gu[1], wv[1, :, cols], FIRST)
        part[1, :, cols] = total.astype(jnp.bfloat16)

    loop(0, D // COLS, back_to_input)
    rc_copy(1).start()

    mine = pl.ds(pl.multiple_of(y * OWN, OWN), OWN)
    other = pl.ds(pl.multiple_of(OWN - y * OWN, OWN), OWN)

    def ry_copy(n):
        return remote(ysend.at[n], yrecv.at[n], ry_s.at[n], ry_r.at[n], across)

    def x_sum(n, side):
        start = pl.multiple_of((core * 4 + x) * PAIR + side * OWN, OWN)
        total = part[n, pl.ds(start, OWN), :].astype(jnp.float32)
        rows = mine if side is y else other
        for j in (1, 2, 3):
            total = total + got[n, j, rows, :].astype(jnp.float32)
        return total

    def across_y(n):
        for j in (1, 2, 3):
            rx_copy(n, j).wait_recv()
        ysend[n] = x_sum(n, 1 - y).astype(jnp.bfloat16)
        ry_copy(n).start()

    across_y(0)
    sum_cores(1)
    spread(2)
    spread(3)
    across_y(1)
    loop(last, BLOCKS, send)
    pass_on(2)
    pass_on(3)

    for a in (2, 3):
        gathered(a)
    for c in raws:
        c.wait_recv()

    def keep_mixed(i, rows, new):
        praw[i, rows, :] = mean(newv[i, rows, :], new)

    def redo(b):
        forward(praw, 2, b)
        backward(praw, 2, b, keep_mixed)
        for i in range(3):
            store(i, praw, 0, 2 * b).start()
            store(i, praw, 0, 2 * b + 1).start()

    loop(0, first, redo)

    ry_copy(0).wait_recv()
    lo_v[...] = ((x_sum(0, y) + yrecv[0].astype(jnp.float32)) * HIDDEN).astype(jnp.bfloat16)
    store_lo = pltpu.make_async_copy(lo_v, lo, load_sem.at[0])
    store_lo.start()
    ry_copy(1).wait_recv()
    d_normed = (x_sum(1, y) + yrecv[1].astype(jnp.float32)) * MODEL
    inner = jnp.mean(d_normed * norm_v[...], axis=-1, keepdims=True)
    value = tok_v[...].astype(jnp.float32)
    inverse = lax.rsqrt(jnp.mean(value * value, axis=-1, keepdims=True) + EPSILON)
    dt_v[...] = (inverse * (d_normed - norm_v[...] * inner)).astype(jnp.bfloat16)
    store_dt = pltpu.make_async_copy(dt_v, dt, load_sem.at[1])
    store_dt.start()

    def mix(q):
        z_new(q).wait_recv()
        for i in range(3):
            rows = piece(q, raw)
            pnew[i, rows, :] = mean(newv[i, piece(q), :], pnew[i, rows, :])
            store(i, pnew, raw, q).start()

    loop(2 * first, 2 * BLOCKS, mix)

    store_lo.wait()
    store_dt.wait()
    for a in range(4):
        y_copy(a).wait_send()
        for j in range(1, 4):
            x_copy(a, j).wait_send()
        for j in range(4):
            c_copy(a, j).wait_send()
    for n in (0, 1):
        rc_copy(n).wait_send()
        for j in (1, 2, 3):
            rx_copy(n, j).wait_send()
        ry_copy(n).wait_send()
        z_tok(n).wait_send()
    for c in raws:
        c.wait_send()
    loop(2 * first, 2 * BLOCKS, lambda q: z_new(q).wait_send())
    for i in range(3):
        loop(0, 2 * first, lambda q: store(i, praw, 0, q).wait())
        loop(2 * first, 2 * BLOCKS, lambda q: store(i, pnew, raw, q).wait())


def exchange(k, tok, cot, gate, up, down):
    raw = RAW[k]
    bf, f32 = jnp.bfloat16, jnp.float32
    dma = pltpu.SemaphoreType.DMA
    weight = jax.ShapeDtypeStruct((ROWS, D), bf)
    small = jax.ShapeDtypeStruct((OWN, D), bf)
    return pl.pallas_call(
        functools.partial(kernel, k, raw),
        out_shape=(weight, weight, weight, small, small),
        in_specs=[HBM] * 5,
        out_specs=(ANY,) * 5,
        scratch_shapes=[
            pltpu.VMEM((OWN, D), bf),
            pltpu.VMEM((OWN, D), f32),
            pltpu.VMEM((4, TOK, D), bf),
            pltpu.VMEM((3, ROWS, D), bf),
            pltpu.VMEM((3, ROWS, D), bf),
            pltpu.VMEM((3, raw, D), bf),
            pltpu.VMEM((3, ROWS - raw, D), bf),
            pltpu.VMEM((ROWS, TOK), f32),
            pltpu.VMEM((ROWS, TOK), f32),
            pltpu.VMEM((ROWS, TOK), bf),
            pltpu.VMEM((2, ROWS, TOK), bf),
            pltpu.VMEM((2, TOK, D), bf),
            pltpu.VMEM((2, TOK // 2, D), bf),
            pltpu.VMEM((2, 4, PAIR, D), bf),
            pltpu.VMEM((2, OWN, D), bf),
            pltpu.VMEM((2, OWN, D), bf),
            pltpu.VMEM((OWN, D), bf),
            pltpu.VMEM((OWN, D), bf),
            dma((5,)),
            dma((3, 2 * BLOCKS)),
            dma((4,)),
            dma((4,)),
            dma((4, 4)),
            dma((4, 4)),
            dma((4, 4)),
            dma((4, 4)),
            dma((2,)),
            dma((2,)),
            dma((2, 4)),
            dma((2, 4)),
            dma((2,)),
            dma((2,)),
            dma((2,)),
            dma((2,)),
            dma((3, BLOCKS)),
            dma((3, BLOCKS)),
            dma((2 * BLOCKS,)),
            dma((2 * BLOCKS,)),
        ],
        compiler_params=pltpu.CompilerParams(
            collective_id=k, has_side_effects=True, vmem_limit_bytes=44 * 1024 * 1024
        ),
        name=f"exchange_{k}",
    )(tok, cot, gate, up, down)


def finish_kernel(*refs):
    arrays, outs, sems = refs[:5], refs[5:10], refs[10]
    copies = [pltpu.make_async_copy(a, o, sems.at[i]) for i, (a, o) in enumerate(zip(arrays, outs))]
    for c in copies:
        c.start()
    for c in copies:
        c.wait()


def finish(arrays):
    return pl.pallas_call(
        finish_kernel,
        out_shape=tuple(jax.ShapeDtypeStruct(a.shape, a.dtype) for a in arrays),
        in_specs=[VMEM] * 5,
        out_specs=(ANY,) * 5,
        scratch_shapes=[pltpu.SemaphoreType.DMA((5,))],
        compiler_params=pltpu.CompilerParams(vmem_limit_bytes=8 * 1024 * 1024),
        name="finish",
    )(*arrays)


def body(tokens_in, cotangent, gate_weight, up_weight, down_weight, step_index):
    k = step_index[0] % 4
    branches = [lambda *args, n=n: finish(exchange(n, *args)) for n in range(4)]
    gate, up, down, lo, dt = lax.switch(
        k, branches, tokens_in, cotangent, gate_weight.T, up_weight.T, down_weight
    )
    return gate.T, up.T, down, lo, dt


def solution(mesh):
    rows = P(("replica", "tensor"), None)
    split = P("replica", "tensor")
    return jax.shard_map(
        body,
        mesh=mesh,
        in_specs=(rows, rows, split, split, rows, P()),
        out_specs=(split, split, rows, rows, rows),
        check_vma=False,
    )
```

```python
import functools

import jax
import jax.numpy as jnp
from jax import lax
from jax.experimental import pallas as pl
from jax.experimental.pallas import tpu as pltpu
from jax.sharding import PartitionSpec as P

D = 2048
FF = 7168
EPSILON = 1e-05
RATE = 2.0
MODEL = D ** (-0.5)
HIDDEN = FF ** (-0.5)

TOK = 512
OWN = 32
PAIR = 64
ROWS = 448
STEP = 64
BLOCKS = ROWS // STEP
PIECE = STEP
PIECES = STEP // PIECE
COLS = 256

MESH = pl.DeviceIdType.MESH
ANY = pl.BlockSpec(memory_space=pl.ANY)
HBM = pl.BlockSpec(memory_space=pltpu.HBM)
VMEM = pl.BlockSpec(memory_space=pltpu.VMEM)

RAW = (192, 128, 128, 256)
HELD = (0, 0, 0, 3)


def dot(a, b, dims):
    return lax.dot_general(a, b, (dims, ((), ())), preferred_element_type=jnp.float32)


LAST = ((1,), (1,))
PLAIN = ((1,), (0,))
FIRST = ((0,), (0,))


def kernel(
    k, raw,
    tok, cot, gate, up, down,
    mixed_gate, mixed_up, mixed_down, lo, dt,
    tok_v, norm_v, gath, wv, newv, praw, pnew,
    act_a, act_b, hid, d_gu, part, half, got, ysend, yrecv, lo_v, dt_v,
    load_sem, store_sem,
    gy_s, gy_r, gx_s, gx_r, gc_s, gc_r,
    rc_s, rc_r, rx_s, rx_r, ry_s, ry_r,
    zt_s, zt_r, zraw_s, zraw_r, znew_s, znew_r,
):
    rep, ten = lax.axis_index("replica"), lax.axis_index("tensor")
    core, y, x = lax.rem(ten, 2), lax.rem(ten // 2, 2), ten // 4
    bit = lax.rem(rep // (1 << k), 2)
    partner = (rep + (1 << k) - (2 << k) * bit, ten)
    across = (rep, ten + 2 - 4 * y)
    sibling = (rep, ten + 1 - 2 * core)
    crossed = k == 3
    beside = (partner[0], across[1]) if crossed else partner
    mixed = (mixed_gate, mixed_up, mixed_down)

    def along_x(j):
        return (rep, lax.rem(x + j, 4) * 4 + y * 2 + core)

    def pair_rows(c, xx):
        return pl.ds(pl.multiple_of((c * 4 + xx) * PAIR, PAIR), PAIR)

    own_rows = pl.ds(pl.multiple_of((core * 4 + x) * PAIR + y * OWN, OWN), OWN)
    across_rows = pl.ds(pl.multiple_of((core * 4 + x) * PAIR + OWN - y * OWN, OWN), OWN)

    def remote(src, dst, send, recv, device):
        return pltpu.make_async_remote_copy(
            src_ref=src, dst_ref=dst, send_sem=send, recv_sem=recv, device_id=device, device_id_type=MESH
        )

    load_tok = pltpu.make_async_copy(tok, tok_v, load_sem.at[0])
    load_cot = pltpu.make_async_copy(cot, gath.at[1, own_rows], load_sem.at[1])
    load_w = [
        pltpu.make_async_copy(ref, wv.at[i], load_sem.at[2 + i]) for i, ref in enumerate((gate, up, down))
    ]
    barrier = pltpu.get_barrier_semaphore()
    friends = [partner, across, sibling] + [along_x(j) for j in (1, 2, 3)] + [beside] * crossed
    for device in friends:
        pl.semaphore_signal(barrier, inc=1, device_id=device, device_id_type=MESH)
    load_tok.start()
    load_cot.start()
    for c in load_w:
        c.start()
    pl.semaphore_wait(barrier, len(friends))

    first = raw // STEP
    raws = [
        remote(ref.at[pl.ds(0, raw)], praw.at[i], zraw_s.at[i], zraw_r.at[i], partner)
        for i, ref in enumerate((gate, up, down))
    ]
    if not crossed:
        raws[0].start()

    load_tok.wait()
    value = tok_v[...].astype(jnp.float32)
    inverse = lax.rsqrt(jnp.mean(value * value, axis=-1, keepdims=True) + EPSILON)
    norm_v[...] = value * inverse
    gath[0, own_rows, :] = norm_v[...].astype(jnp.bfloat16)
    load_cot.wait()

    def y_copy(a):
        rows = across_rows if crossed and a >= 2 else own_rows
        return remote(gath.at[a, rows], gath.at[a, rows], gy_s.at[a], gy_r.at[a], across)

    def x_copy(a, j):
        rows = pair_rows(core, x)
        return remote(gath.at[a, rows], gath.at[a, rows], gx_s.at[a, j], gx_r.at[a, j], along_x(j))

    def c_copy(a, j):
        rows = pair_rows(core, lax.rem(x + 4 - j, 4))
        return remote(gath.at[a, rows], gath.at[a, rows], gc_s.at[a, j], gc_r.at[a, j], sibling)

    def spread(a):
        y_copy(a).wait_recv()
        for j in (1, 3, 2):
            x_copy(a, j).start()
        c_copy(a, 0).start()

    def pass_on(a):
        for j in (1, 3, 2):
            x_copy(a, j).wait_recv()
            c_copy(a, j).start()

    def gathered(a):
        for j in range(4):
            c_copy(a, j).wait_recv()

    y_copy(0).start()
    y_copy(1).start()

    def z_tok(a):
        return remote(gath.at[a, own_rows], gath.at[a + 2, own_rows], zt_s.at[a], zt_r.at[a], beside)

    def block(b):
        return pl.ds(pl.multiple_of(b * STEP, STEP), STEP)

    def piece(q, low=0):
        return pl.ds(pl.multiple_of(q * PIECE - low, PIECE), PIECE)

    def z_new(q):
        return remote(newv.at[:, piece(q)], pnew.at[:, piece(q, raw)], znew_s.at[q], znew_r.at[q], partner)

    def store(i, ref, low, q):
        return pltpu.make_async_copy(ref.at[i, piece(q, low)], mixed[i].at[piece(q)], store_sem.at[i, q])

    def partner_tokens():
        for a in (0, 1):
            z_tok(a).wait_recv()
            y_copy(a + 2).start()

    z_tok(0).start()
    z_tok(1).start()
    if crossed:
        partner_tokens()
    for c in raws[0 if crossed else 1:]:
        c.start()
    spread(0)
    spread(1)
    pass_on(0)
    gathered(0)
    for c in load_w:
        c.wait()

    def forward(w, base, b):
        rows = block(b)
        gate_pre = dot(w[0, rows, :], gath[base], LAST) * MODEL
        up_pre = dot(w[1, rows, :], gath[base], LAST) * MODEL
        s = jax.nn.sigmoid(gate_pre)
        silu = gate_pre * s
        hid[rows, :] = (silu * up_pre).astype(jnp.bfloat16)
        act_a[rows, :] = up_pre * s * (1.0 + gate_pre * (1.0 - s))
        act_b[rows, :] = silu

    def backward(w, base, b, keep):
        rows = block(b)
        d_hidden = dot(w[2, rows, :], gath[base + 1], LAST) * HIDDEN
        d_gu[0, rows, :] = (d_hidden * act_a[rows, :]).astype(jnp.bfloat16)
        d_gu[1, rows, :] = (d_hidden * act_b[rows, :]).astype(jnp.bfloat16)
        for i, (left, right, scale) in enumerate(
            ((d_gu.at[0], base, MODEL), (d_gu.at[1], base, MODEL), (hid, base + 1, HIDDEN))
        ):
            grad = dot(left[rows, :], gath[right], PLAIN) * scale
            keep(i, rows, (w[i, rows, :].astype(jnp.float32) - RATE * grad).astype(jnp.bfloat16))

    def keep_own(i, rows, new):
        newv[i, rows, :] = new

    def mean(a, b):
        return (0.5 * (a.astype(jnp.float32) + b.astype(jnp.float32))).astype(jnp.bfloat16)

    def loop(low, high, step):
        if high > low:
            lax.fori_loop(low, high, lambda b, _: (step(b), 0)[1], 0)

    loop(0, BLOCKS, lambda b: forward(wv, 0, b))
    pass_on(1)

    def core_rows(c):
        return pl.ds(pl.multiple_of(c * (TOK // 2), TOK // 2), TOK // 2)

    def rc_copy(n):
        return remote(part.at[n, core_rows(1 - core)], half.at[n], rc_s.at[n], rc_r.at[n], sibling)

    def rx_copy(n, j):
        rows = pair_rows(core, lax.rem(x + j, 4))
        return remote(part.at[n, rows], got.at[n, j], rx_s.at[n, j], rx_r.at[n, j], along_x(j))

    def sum_cores(n):
        rc_copy(n).wait_recv()
        rows = core_rows(core)
        total = part[n, rows, :].astype(jnp.float32) + half[n].astype(jnp.float32)
        part[n, rows, :] = total.astype(jnp.bfloat16)
        for j in (2, 1, 3):
            rx_copy(n, j).start()

    def layer(n):
        cols = pl.ds(pl.multiple_of(n * COLS, COLS), COLS)
        part[0, :, cols] = dot(hid[...], wv[2, :, cols], FIRST).astype(jnp.bfloat16)

    loop(0, D // COLS, layer)
    rc_copy(0).start()

    gathered(1)

    def send(b):
        for q in range(PIECES):
            z_new(PIECES * b + q).start()

    def update_and_send(b):
        backward(wv, 0, b, keep_own)
        send(b)

    last = BLOCKS - HELD[k]
    loop(first, last, update_and_send)
    loop(last, BLOCKS, lambda b: backward(wv, 0, b, keep_own))
    sum_cores(0)
    if not crossed:
        partner_tokens()
    loop(0, first, lambda b: backward(wv, 0, b, keep_own))

    def back_to_input(n):
        cols = pl.ds(pl.multiple_of(n * COLS, COLS), COLS)
        total = dot(d_gu[0], wv[0, :, cols], FIRST) + dot(d_gu[1], wv[1, :, cols], FIRST)
        part[1, :, cols] = total.astype(jnp.bfloat16)

    loop(0, D // COLS, back_to_input)
    rc_copy(1).start()

    mine = pl.ds(pl.multiple_of(y * OWN, OWN), OWN)
    other = pl.ds(pl.multiple_of(OWN - y * OWN, OWN), OWN)

    def ry_copy(n):
        return remote(ysend.at[n], yrecv.at[n], ry_s.at[n], ry_r.at[n], across)

    def x_sum(n, side):
        start = pl.multiple_of((core * 4 + x) * PAIR + side * OWN, OWN)
        total = part[n, pl.ds(start, OWN), :].astype(jnp.float32)
        rows = mine if side is y else other
        for j in (1, 2, 3):
            total = total + got[n, j, rows, :].astype(jnp.float32)
        return total

    def across_y(n):
        for j in (1, 2, 3):
            rx_copy(n, j).wait_recv()
        ysend[n] = x_sum(n, 1 - y).astype(jnp.bfloat16)
        ry_copy(n).start()

    across_y(0)
    sum_cores(1)
    spread(2)
    spread(3)
    across_y(1)
    loop(last, BLOCKS, send)
    pass_on(2)
    pass_on(3)

    for a in (2, 3):
        gathered(a)
    for c in raws:
        c.wait_recv()

    def keep_mixed(i, rows, new):
        praw[i, rows, :] = mean(newv[i, rows, :], new)

    def redo(b):
        forward(praw, 2, b)
        backward(praw, 2, b, keep_mixed)
        for i in range(3):
            for q in range(PIECES):
                store(i, praw, 0, PIECES * b + q).start()

    loop(0, first, redo)

    ry_copy(0).wait_recv()
    lo_v[...] = ((x_sum(0, y) + yrecv[0].astype(jnp.float32)) * HIDDEN).astype(jnp.bfloat16)
    store_lo = pltpu.make_async_copy(lo_v, lo, load_sem.at[0])
    store_lo.start()
    ry_copy(1).wait_recv()
    d_normed = (x_sum(1, y) + yrecv[1].astype(jnp.float32)) * MODEL
    inner = jnp.mean(d_normed * norm_v[...], axis=-1, keepdims=True)
    value = tok_v[...].astype(jnp.float32)
    inverse = lax.rsqrt(jnp.mean(value * value, axis=-1, keepdims=True) + EPSILON)
    dt_v[...] = (inverse * (d_normed - norm_v[...] * inner)).astype(jnp.bfloat16)
    store_dt = pltpu.make_async_copy(dt_v, dt, load_sem.at[1])
    store_dt.start()

    def mix(q):
        z_new(q).wait_recv()
        for i in range(3):
            rows = piece(q, raw)
            pnew[i, rows, :] = mean(newv[i, piece(q), :], pnew[i, rows, :])
            store(i, pnew, raw, q).start()

    loop(PIECES * first, PIECES * BLOCKS, mix)

    store_lo.wait()
    store_dt.wait()
    for a in range(4):
        y_copy(a).wait_send()
        for j in range(1, 4):
            x_copy(a, j).wait_send()
        for j in range(4):
            c_copy(a, j).wait_send()
    for n in (0, 1):
        rc_copy(n).wait_send()
        for j in (1, 2, 3):
            rx_copy(n, j).wait_send()
        ry_copy(n).wait_send()
        z_tok(n).wait_send()
    for c in raws:
        c.wait_send()
    loop(PIECES * first, PIECES * BLOCKS, lambda q: z_new(q).wait_send())
    for i in range(3):
        loop(0, PIECES * first, lambda q: store(i, praw, 0, q).wait())
        loop(PIECES * first, PIECES * BLOCKS, lambda q: store(i, pnew, raw, q).wait())


def exchange(k, tok, cot, gate, up, down):
    raw = RAW[k]
    bf, f32 = jnp.bfloat16, jnp.float32
    dma = pltpu.SemaphoreType.DMA
    weight = jax.ShapeDtypeStruct((ROWS, D), bf)
    small = jax.ShapeDtypeStruct((OWN, D), bf)
    return pl.pallas_call(
        functools.partial(kernel, k, raw),
        out_shape=(weight, weight, weight, small, small),
        in_specs=[HBM] * 5,
        out_specs=(ANY,) * 5,
        scratch_shapes=[
            pltpu.VMEM((OWN, D), bf),
            pltpu.VMEM((OWN, D), f32),
            pltpu.VMEM((4, TOK, D), bf),
            pltpu.VMEM((3, ROWS, D), bf),
            pltpu.VMEM((3, ROWS, D), bf),
            pltpu.VMEM((3, raw, D), bf),
            pltpu.VMEM((3, ROWS - raw, D), bf),
            pltpu.VMEM((ROWS, TOK), f32),
            pltpu.VMEM((ROWS, TOK), f32),
            pltpu.VMEM((ROWS, TOK), bf),
            pltpu.VMEM((2, ROWS, TOK), bf),
            pltpu.VMEM((2, TOK, D), bf),
            pltpu.VMEM((2, TOK // 2, D), bf),
            pltpu.VMEM((2, 4, PAIR, D), bf),
            pltpu.VMEM((2, OWN, D), bf),
            pltpu.VMEM((2, OWN, D), bf),
            pltpu.VMEM((OWN, D), bf),
            pltpu.VMEM((OWN, D), bf),
            dma((5,)),
            dma((3, PIECES * BLOCKS)),
            dma((4,)),
            dma((4,)),
            dma((4, 4)),
            dma((4, 4)),
            dma((4, 4)),
            dma((4, 4)),
            dma((2,)),
            dma((2,)),
            dma((2, 4)),
            dma((2, 4)),
            dma((2,)),
            dma((2,)),
            dma((2,)),
            dma((2,)),
            dma((3,)),
            dma((3,)),
            dma((PIECES * BLOCKS,)),
            dma((PIECES * BLOCKS,)),
        ],
        compiler_params=pltpu.CompilerParams(
            collective_id=k, has_side_effects=True, vmem_limit_bytes=44 * 1024 * 1024
        ),
        name=f"exchange_{k}",
    )(tok, cot, gate, up, down)


def finish_kernel(*refs):
    arrays, outs, sems = refs[:5], refs[5:10], refs[10]
    copies = [pltpu.make_async_copy(a, o, sems.at[i]) for i, (a, o) in enumerate(zip(arrays, outs))]
    for c in copies:
        c.start()
    for c in copies:
        c.wait()


def finish(arrays):
    return pl.pallas_call(
        finish_kernel,
        out_shape=tuple(jax.ShapeDtypeStruct(a.shape, a.dtype) for a in arrays),
        in_specs=[VMEM] * 5,
        out_specs=(ANY,) * 5,
        scratch_shapes=[pltpu.SemaphoreType.DMA((5,))],
        compiler_params=pltpu.CompilerParams(vmem_limit_bytes=8 * 1024 * 1024),
        name="finish",
    )(*arrays)


def body(tokens_in, cotangent, gate_weight, up_weight, down_weight, step_index):
    k = step_index[0] % 4
    branches = [lambda *args, n=n: finish(exchange(n, *args)) for n in range(4)]
    gate, up, down, lo, dt = lax.switch(
        k, branches, tokens_in, cotangent, gate_weight.T, up_weight.T, down_weight
    )
    return gate.T, up.T, down, lo, dt


def solution(mesh):
    rows = P(("replica", "tensor"), None)
    split = P("replica", "tensor")
    return jax.shard_map(
        body,
        mesh=mesh,
        in_specs=(rows, rows, split, split, rows, P()),
        out_specs=(split, split, rows, rows, rows),
        check_vma=False,
    )
```

```python
import functools

import jax
import jax.numpy as jnp
from jax import lax
from jax.experimental import pallas as pl
from jax.experimental.pallas import tpu as pltpu
from jax.sharding import PartitionSpec as P

D = 2048
FF = 7168
EPSILON = 1e-05
RATE = 2.0
MODEL = D ** (-0.5)
HIDDEN = FF ** (-0.5)

TOK = 512
OWN = 32
PAIR = 64
ROWS = 448
STEP = 64
BLOCKS = ROWS // STEP
PIECE = STEP
PIECES = STEP // PIECE
COLS = 256

MESH = pl.DeviceIdType.MESH
ANY = pl.BlockSpec(memory_space=pl.ANY)
HBM = pl.BlockSpec(memory_space=pltpu.HBM)
VMEM = pl.BlockSpec(memory_space=pltpu.VMEM)

RAW = (192, 128, 128, 256)
HELD = (0, 0, 0, 3)


def dot(a, b, dims):
    return lax.dot_general(a, b, (dims, ((), ())), preferred_element_type=jnp.float32)


LAST = ((1,), (1,))
PLAIN = ((1,), (0,))
FIRST = ((0,), (0,))


def kernel(
    k, raw,
    tok, cot, gate, up, down,
    mixed_gate, mixed_up, mixed_down, lo, dt,
    tok_v, norm_v, gath, wv, newv, praw, pnew,
    act_a, act_b, hid, d_gu, part, half, got, ysend, yrecv,
    load_sem,
    gy_s, gy_r, gx_s, gx_r, gc_s, gc_r,
    rc_s, rc_r, rx_s, rx_r, ry_s, ry_r,
    zt_s, zt_r, zraw_s, zraw_r, znew_s, znew_r,
):
    rep, ten = lax.axis_index("replica"), lax.axis_index("tensor")
    core, y, x = lax.rem(ten, 2), lax.rem(ten // 2, 2), ten // 4
    bit = lax.rem(rep // (1 << k), 2)
    partner = (rep + (1 << k) - (2 << k) * bit, ten)
    across = (rep, ten + 2 - 4 * y)
    sibling = (rep, ten + 1 - 2 * core)
    crossed = k == 3
    beside = (partner[0], across[1]) if crossed else partner
    mixed = (mixed_gate, mixed_up, mixed_down)

    def along_x(j):
        return (rep, lax.rem(x + j, 4) * 4 + y * 2 + core)

    def pair_rows(c, xx):
        return pl.ds(pl.multiple_of((c * 4 + xx) * PAIR, PAIR), PAIR)

    own_rows = pl.ds(pl.multiple_of((core * 4 + x) * PAIR + y * OWN, OWN), OWN)
    across_rows = pl.ds(pl.multiple_of((core * 4 + x) * PAIR + OWN - y * OWN, OWN), OWN)

    def remote(src, dst, send, recv, device):
        return pltpu.make_async_remote_copy(
            src_ref=src, dst_ref=dst, send_sem=send, recv_sem=recv, device_id=device, device_id_type=MESH
        )

    load_tok = pltpu.make_async_copy(tok, tok_v, load_sem.at[0])
    load_cot = pltpu.make_async_copy(cot, gath.at[1, own_rows], load_sem.at[1])
    load_w = [
        pltpu.make_async_copy(ref, wv.at[i], load_sem.at[2 + i]) for i, ref in enumerate((gate, up, down))
    ]
    barrier = pltpu.get_barrier_semaphore()
    friends = [partner, across, sibling] + [along_x(j) for j in (1, 2, 3)] + [beside] * crossed
    for device in friends:
        pl.semaphore_signal(barrier, inc=1, device_id=device, device_id_type=MESH)
    load_tok.start()
    load_cot.start()
    for c in load_w:
        c.start()
    pl.semaphore_wait(barrier, len(friends))

    first = raw // STEP
    raws = [
        remote(ref.at[pl.ds(0, raw)], praw.at[i], zraw_s.at[i], zraw_r.at[i], partner)
        for i, ref in enumerate((gate, up, down))
    ]
    if not crossed:
        raws[0].start()

    def y_copy(a):
        rows = across_rows if crossed and a >= 2 else own_rows
        return remote(gath.at[a, rows], gath.at[a, rows], gy_s.at[a], gy_r.at[a], across)

    def x_copy(a, j):
        rows = pair_rows(core, x)
        return remote(gath.at[a, rows], gath.at[a, rows], gx_s.at[a, j], gx_r.at[a, j], along_x(j))

    def c_copy(a, j):
        rows = pair_rows(core, lax.rem(x + 4 - j, 4))
        return remote(gath.at[a, rows], gath.at[a, rows], gc_s.at[a, j], gc_r.at[a, j], sibling)

    def spread(a):
        y_copy(a).wait_recv()
        for j in (1, 3, 2):
            x_copy(a, j).start()
        c_copy(a, 0).start()

    def pass_on(a):
        for j in (1, 3, 2):
            x_copy(a, j).wait_recv()
            c_copy(a, j).start()

    def gathered(a):
        for j in range(4):
            c_copy(a, j).wait_recv()

    def z_tok(a):
        return remote(gath.at[a, own_rows], gath.at[a + 2, own_rows], zt_s.at[a], zt_r.at[a], beside)

    def block(b):
        return pl.ds(pl.multiple_of(b * STEP, STEP), STEP)

    def piece(q, low=0):
        return pl.ds(pl.multiple_of(q * PIECE - low, PIECE), PIECE)

    def z_new(q):
        return remote(newv.at[:, piece(q)], pnew.at[:, piece(q, raw)], znew_s.at[q], znew_r.at[q], partner)

    def partner_tokens():
        for a in (1, 0):
            z_tok(a).wait_recv()
            y_copy(a + 2).start()

    load_cot.wait()
    y_copy(1).start()
    z_tok(1).start()
    load_tok.wait()
    value = tok_v[...].astype(jnp.float32)
    inverse = lax.rsqrt(jnp.mean(value * value, axis=-1, keepdims=True) + EPSILON)
    norm_v[...] = value * inverse
    gath[0, own_rows, :] = norm_v[...].astype(jnp.bfloat16)
    y_copy(0).start()
    z_tok(0).start()
    if crossed:
        partner_tokens()
    for c in raws[0 if crossed else 1:]:
        c.start()
    spread(0)
    spread(1)
    pass_on(0)
    gathered(0)
    for c in load_w:
        c.wait()

    def forward(w, base, b):
        rows = block(b)
        gate_pre = dot(w[0, rows, :], gath[base], LAST) * MODEL
        up_pre = dot(w[1, rows, :], gath[base], LAST) * MODEL
        s = jax.nn.sigmoid(gate_pre)
        silu = gate_pre * s
        hid[rows, :] = (silu * up_pre).astype(jnp.bfloat16)
        act_a[rows, :] = up_pre * s * (1.0 + gate_pre * (1.0 - s))
        act_b[rows, :] = silu

    def backward(w, base, b, keep):
        rows = block(b)
        d_hidden = dot(w[2, rows, :], gath[base + 1], LAST) * HIDDEN
        d_gu[0, rows, :] = (d_hidden * act_a[rows, :]).astype(jnp.bfloat16)
        d_gu[1, rows, :] = (d_hidden * act_b[rows, :]).astype(jnp.bfloat16)
        for i, (left, right, scale) in enumerate(
            ((d_gu.at[0], base, MODEL), (d_gu.at[1], base, MODEL), (hid, base + 1, HIDDEN))
        ):
            grad = dot(left[rows, :], gath[right], PLAIN) * scale
            keep(i, rows, (w[i, rows, :].astype(jnp.float32) - RATE * grad).astype(jnp.bfloat16))

    def keep_own(i, rows, new):
        newv[i, rows, :] = new

    def mean(a, b):
        return (0.5 * (a.astype(jnp.float32) + b.astype(jnp.float32))).astype(jnp.bfloat16)

    def loop(low, high, step):
        if high > low:
            lax.fori_loop(low, high, lambda b, _: (step(b), 0)[1], 0)

    loop(0, BLOCKS, lambda b: forward(wv, 0, b))
    pass_on(1)

    def core_rows(c):
        return pl.ds(pl.multiple_of(c * (TOK // 2), TOK // 2), TOK // 2)

    def rc_copy(n):
        return remote(part.at[n, core_rows(1 - core)], half.at[n], rc_s.at[n], rc_r.at[n], sibling)

    def rx_copy(n, j):
        rows = pair_rows(core, lax.rem(x + j, 4))
        return remote(part.at[n, rows], got.at[n, j], rx_s.at[n, j], rx_r.at[n, j], along_x(j))

    def sum_cores(n):
        rc_copy(n).wait_recv()
        rows = core_rows(core)
        total = part[n, rows, :].astype(jnp.float32) + half[n].astype(jnp.float32)
        part[n, rows, :] = total.astype(jnp.bfloat16)
        for j in (2, 1, 3):
            rx_copy(n, j).start()

    def layer(n):
        cols = pl.ds(pl.multiple_of(n * COLS, COLS), COLS)
        part[0, :, cols] = dot(hid[...], wv[2, :, cols], FIRST).astype(jnp.bfloat16)

    loop(0, D // COLS, layer)
    rc_copy(0).start()

    gathered(1)

    def send(b):
        for q in range(PIECES):
            z_new(PIECES * b + q).start()

    def update_and_send(b):
        backward(wv, 0, b, keep_own)
        send(b)

    last = BLOCKS - HELD[k]
    loop(first, last, update_and_send)
    loop(last, BLOCKS, lambda b: backward(wv, 0, b, keep_own))
    sum_cores(0)
    if not crossed:
        partner_tokens()
    loop(0, first, lambda b: backward(wv, 0, b, keep_own))

    def back_to_input(n):
        cols = pl.ds(pl.multiple_of(n * COLS, COLS), COLS)
        total = dot(d_gu[0], wv[0, :, cols], FIRST) + dot(d_gu[1], wv[1, :, cols], FIRST)
        part[1, :, cols] = total.astype(jnp.bfloat16)

    loop(0, D // COLS, back_to_input)
    rc_copy(1).start()

    mine = pl.ds(pl.multiple_of(y * OWN, OWN), OWN)
    other = pl.ds(pl.multiple_of(OWN - y * OWN, OWN), OWN)

    def ry_copy(n):
        return remote(ysend.at[n], yrecv.at[n], ry_s.at[n], ry_r.at[n], across)

    def x_sum(n, side):
        start = pl.multiple_of((core * 4 + x) * PAIR + side * OWN, OWN)
        total = part[n, pl.ds(start, OWN), :].astype(jnp.float32)
        rows = mine if side is y else other
        for j in (1, 2, 3):
            total = total + got[n, j, rows, :].astype(jnp.float32)
        return total

    def across_y(n):
        for j in (1, 2, 3):
            rx_copy(n, j).wait_recv()
        ysend[n] = x_sum(n, 1 - y).astype(jnp.bfloat16)
        ry_copy(n).start()

    across_y(0)
    sum_cores(1)
    spread(2)
    spread(3)
    across_y(1)
    loop(last, BLOCKS, send)
    pass_on(2)
    pass_on(3)

    for a in (2, 3):
        gathered(a)
    for c in raws:
        c.wait_recv()

    def keep_mixed(i, rows, new):
        mixed[i][rows, :] = mean(newv[i, rows, :], new)

    def redo(b):
        forward(praw, 2, b)
        backward(praw, 2, b, keep_mixed)

    loop(0, first, redo)

    ry_copy(0).wait_recv()
    lo[...] = ((x_sum(0, y) + yrecv[0].astype(jnp.float32)) * HIDDEN).astype(jnp.bfloat16)
    ry_copy(1).wait_recv()
    d_normed = (x_sum(1, y) + yrecv[1].astype(jnp.float32)) * MODEL
    inner = jnp.mean(d_normed * norm_v[...], axis=-1, keepdims=True)
    value = tok_v[...].astype(jnp.float32)
    inverse = lax.rsqrt(jnp.mean(value * value, axis=-1, keepdims=True) + EPSILON)
    dt[...] = (inverse * (d_normed - norm_v[...] * inner)).astype(jnp.bfloat16)

    def mix(q):
        z_new(q).wait_recv()
        for i in range(3):
            mixed[i][piece(q), :] = mean(newv[i, piece(q), :], pnew[i, piece(q, raw), :])

    loop(PIECES * first, PIECES * BLOCKS, mix)

    for a in range(4):
        y_copy(a).wait_send()
        for j in range(1, 4):
            x_copy(a, j).wait_send()
        for j in range(4):
            c_copy(a, j).wait_send()
    for n in (0, 1):
        rc_copy(n).wait_send()
        for j in (1, 2, 3):
            rx_copy(n, j).wait_send()
        ry_copy(n).wait_send()
        z_tok(n).wait_send()
    for c in raws:
        c.wait_send()
    loop(PIECES * first, PIECES * BLOCKS, lambda q: z_new(q).wait_send())


def exchange(k, tok, cot, gate, up, down):
    raw = RAW[k]
    bf, f32 = jnp.bfloat16, jnp.float32
    dma = pltpu.SemaphoreType.DMA
    weight = jax.ShapeDtypeStruct((ROWS, D), bf)
    small = jax.ShapeDtypeStruct((OWN, D), bf)
    return pl.pallas_call(
        functools.partial(kernel, k, raw),
        out_shape=(weight, weight, weight, small, small),
        in_specs=[HBM] * 5,
        out_specs=(VMEM,) * 5,
        scratch_shapes=[
            pltpu.VMEM((OWN, D), bf),
            pltpu.VMEM((OWN, D), f32),
            pltpu.VMEM((4, TOK, D), bf),
            pltpu.VMEM((3, ROWS, D), bf),
            pltpu.VMEM((3, ROWS, D), bf),
            pltpu.VMEM((3, raw, D), bf),
            pltpu.VMEM((3, ROWS - raw, D), bf),
            pltpu.VMEM((ROWS, TOK), f32),
            pltpu.VMEM((ROWS, TOK), f32),
            pltpu.VMEM((ROWS, TOK), bf),
            pltpu.VMEM((2, ROWS, TOK), bf),
            pltpu.VMEM((2, TOK, D), bf),
            pltpu.VMEM((2, TOK // 2, D), bf),
            pltpu.VMEM((2, 4, PAIR, D), bf),
            pltpu.VMEM((2, OWN, D), bf),
            pltpu.VMEM((2, OWN, D), bf),
            dma((5,)),
            dma((4,)),
            dma((4,)),
            dma((4, 4)),
            dma((4, 4)),
            dma((4, 4)),
            dma((4, 4)),
            dma((2,)),
            dma((2,)),
            dma((2, 4)),
            dma((2, 4)),
            dma((2,)),
            dma((2,)),
            dma((2,)),
            dma((2,)),
            dma((3,)),
            dma((3,)),
            dma((PIECES * BLOCKS,)),
            dma((PIECES * BLOCKS,)),
        ],
        compiler_params=pltpu.CompilerParams(
            collective_id=k, has_side_effects=True, vmem_limit_bytes=44 * 1024 * 1024
        ),
        name=f"exchange_{k}",
    )(tok, cot, gate, up, down)


def finish_kernel(*refs):
    arrays, outs, sems = refs[:5], refs[5:10], refs[10]
    copies = [pltpu.make_async_copy(a, o, sems.at[i]) for i, (a, o) in enumerate(zip(arrays, outs))]
    for c in copies:
        c.start()
    for c in copies:
        c.wait()


def finish(arrays):
    return pl.pallas_call(
        finish_kernel,
        out_shape=tuple(jax.ShapeDtypeStruct(a.shape, a.dtype) for a in arrays),
        in_specs=[VMEM] * 5,
        out_specs=(ANY,) * 5,
        scratch_shapes=[pltpu.SemaphoreType.DMA((5,))],
        compiler_params=pltpu.CompilerParams(vmem_limit_bytes=8 * 1024 * 1024),
        name="finish",
    )(*arrays)


def body(tokens_in, cotangent, gate_weight, up_weight, down_weight, step_index):
    k = step_index[0] % 4
    branches = [lambda *args, n=n: finish(exchange(n, *args)) for n in range(4)]
    gate, up, down, lo, dt = lax.switch(
        k, branches, tokens_in, cotangent, gate_weight.T, up_weight.T, down_weight
    )
    return gate.T, up.T, down, lo, dt


def solution(mesh):
    rows = P(("replica", "tensor"), None)
    split = P("replica", "tensor")
    return jax.shard_map(
        body,
        mesh=mesh,
        in_specs=(rows, rows, split, split, rows, P()),
        out_specs=(split, split, rows, rows, rows),
        check_vma=False,
    )
```
